256 devices in a mesh: rep: 32 (over x_lo, z, core), tp: 8 (over x_hi, y).
Axes of the slice: x: 4 (x_hi: 2, x_lo: 2; x = x_hi * 2 + x_lo), y: 4, z: 8, core: 2. Of those that a mesh axis runs over, the one named last changes fastest.
Arguments:
- prefill_x: bfloat16 [8192, 8192], P('rep', 'tp'), as said below
- decode_x: bfloat16 [48, 8192], P(None, 'tp'), as said below
- query_weight: bfloat16 [8192, 8192], P('rep', 'tp'), may hold values from -0.125 to 0.125
- keyvalue_weight: bfloat16 [8192, 2048], P('rep', 'tp'), may hold values from -0.0625 to 0.0625
- key_cache: bfloat16 [48, 4096, 1024], P(None, 'rep', 'tp'), as said below
- value_cache: bfloat16 [48, 4096, 1024], P(None, 'rep', 'tp'), may hold values from -6 to 6
- cache_lengths: int32 [48], replicated, may hold values from 1 to 4096, as said below
- chain_order: int32 [32], replicated, may hold values from 0 to 31, each once
Outputs:
- prefill_attn: bfloat16 [8192, 8192], P('rep', 'tp')
- decode_attn: bfloat16 [48, 8192], P(None, 'tp')
The draws below stay inside these ranges and needn't reach their ends.
Inputs may be any that keep to these rules, and one draw needn't show every extreme that they name: `cache_lengths`: every decode row holds 1 to 4096 cached positions, and some row holds exactly 4096. `chain_order`: each stored block appears once. `prefill_x`: of order one. `decode_x`: of order one. `key_cache`: of order one.
All inputs are finite; a program needn't handle non-finite values.
Results may differ from the reference program's by a relative error of at most 0.012.
The reference program's roundings to bfloat16 on the way count: a program that leaves them out, or rounds other values in their place, can miss the bound.
Values may be sent and summed in bfloat16 or wider, within the bound.
No kernel may reach another device: no remote copies, remote signals or barrier semaphores. Data moves between devices by JAX's collectives and lax.ppermute only.
A program may use at most 128 MiB of HBM per device.

```python
import math
import jax
import jax.numpy as jnp
from jax import lax

D = 8192
HD = 128
HQ = 64
KVH = 8
SEQ_LEN = 128
BATCH = 48
GROUPS = 32
BLOCK_ROWS = 256
TOKENS = 8192
CACHE_LEN = 4096
N_REP = 32


def scaled_rows(key, shape):
    first = jax.random.fold_in(key, 0)
    base = jnp.clip(jax.random.normal(first, shape, jnp.float32), -6.0, 6.0)
    return base


def draw_prefill_x(key, part):
    key = jax.random.fold_in(key, 11)
    return scaled_rows(key, (TOKENS, D)).astype(jnp.bfloat16)


def draw_decode_x(key, part):
    key = jax.random.fold_in(key, 12)
    return scaled_rows(key, (BATCH, D)).astype(jnp.bfloat16)


def draw_key_cache(key, part):
    key = jax.random.fold_in(key, 13)
    return scaled_rows(key, (BATCH, CACHE_LEN, KVH * HD)).astype(jnp.bfloat16)


def draw_cache_lengths(key, part):
    key = jax.random.fold_in(key, 14)
    first, second = jax.random.split(key)
    lengths = jax.random.randint(first, (BATCH,), 1, CACHE_LEN + 1, dtype=jnp.int32)
    longest = jax.random.randint(second, (), 0, BATCH, dtype=jnp.int32)
    return jnp.where(jnp.arange(BATCH, dtype=jnp.int32) == longest, CACHE_LEN, lengths).astype(jnp.int32)


def steps_of(key, extent, cuts, low, high):
    factor_of, own = 1.0, jax.random.fold_in(key, 6)
    for position, shards_of in cuts:
        heights = jnp.exp(jax.random.uniform(jax.random.fold_in(own, position), (shards_of,), jnp.float32, low / len(cuts), high / len(cuts)))
        factor_of = factor_of * jnp.repeat(heights, extent[position] // shards_of).reshape([-1 if axis == position else 1 for axis in range(len(extent))])
    return factor_of


def scatter_about(own_key, shape, width, bound, cuts=(), kind=jnp.bfloat16):
    result = width * jax.random.normal(own_key, shape, jnp.float32)
    if cuts:
        result = result * steps_of(own_key, shape, cuts, -0.22, 0.18)
    return jnp.clip(result, -bound, bound).astype(kind)


def setup_inputs(seed: int = 0) -> dict:
    arg_keys = jax.random.split(jax.random.key(seed), 9)
    prefill_x = draw_prefill_x(jax.random.fold_in(arg_keys[8], 71), 0)
    decode_x = draw_decode_x(jax.random.fold_in(arg_keys[8], 71), 0)
    query_weight = scatter_about(arg_keys[2], (D, HQ * HD), (D // 4) ** -0.5, 0.125, ((0, 32), (1, 8)))
    keyvalue_weight = scatter_about(arg_keys[3], (D, 2 * KVH * HD), D ** -0.5, 0.0625, ((0, 32), (1, 8)))
    key_cache = draw_key_cache(jax.random.fold_in(arg_keys[8], 71), 0)
    value_cache = scatter_about(arg_keys[5], (BATCH, CACHE_LEN, KVH * HD), 1.0, 6.0, ((1, 32), (2, 8)))
    cache_lengths = draw_cache_lengths(jax.random.fold_in(arg_keys[8], 71), 0)
    chain_order = jax.random.permutation(arg_keys[7], GROUPS).astype(jnp.int32)
    return {"prefill_x": prefill_x, "decode_x": decode_x, "query_weight": query_weight, "keyvalue_weight": keyvalue_weight, "key_cache": key_cache, "value_cache": value_cache, "cache_lengths": cache_lengths, "chain_order": chain_order}


def prefill_attention(queries, keyvalues):
    token_rows = queries.shape[0]
    seq_count = token_rows // SEQ_LEN
    query_blocks = queries.astype(jnp.float32).reshape(seq_count, SEQ_LEN, KVH, HQ // KVH, HD)
    pairs = keyvalues.astype(jnp.float32).reshape(seq_count, SEQ_LEN, KVH, 2, HD)
    scores = jnp.einsum('nqhgd,nkhd->nhgqk', query_blocks, pairs[:, :, :, 0]) / math.sqrt(HD)
    causal = jnp.arange(SEQ_LEN)[:, None] >= jnp.arange(SEQ_LEN)[None, :]
    scores = jnp.where(causal, scores, -jnp.inf)
    highest = lax.optimization_barrier(jnp.max(scores, axis=-1, keepdims=True))
    expos = jnp.where(causal, jnp.exp(scores - highest), 0.0)
    sums = lax.optimization_barrier(jnp.sum(expos, axis=-1))
    rounded = expos.astype(jnp.bfloat16).astype(jnp.float32)
    weighted = jnp.einsum('nhgqk,nkhd->nhgqd', rounded, pairs[:, :, :, 1]) / sums[..., None]
    return weighted.astype(jnp.bfloat16).transpose(0, 3, 1, 2, 4).reshape(token_rows, HQ * HD)

def decode_head(head_index, query_all, new_all, key_cache, value_cache, lengths):
    grouped = HQ // KVH
    queries = lax.dynamic_slice_in_dim(query_all, head_index * grouped, grouped, 1).astype(jnp.float32)
    own_pair = lax.dynamic_slice_in_dim(new_all, head_index, 1, 1)[:, 0].astype(jnp.float32)
    cached_keys = lax.dynamic_slice_in_dim(key_cache, head_index * HD, HD, 2).astype(jnp.float32)
    cached_values = lax.dynamic_slice_in_dim(value_cache, head_index * HD, HD, 2).astype(jnp.float32)
    scores = jnp.einsum('bgd,bpd->bgp', queries, cached_keys) / math.sqrt(HD)
    own = jnp.einsum('bgd,bd->bg', queries, own_pair[:, 0]) / math.sqrt(HD)
    allowed = (jnp.arange(CACHE_LEN, dtype=jnp.int32)[None, :] < lengths[:, None])[:, None, :]
    highest = jnp.maximum(lax.optimization_barrier(jnp.max(jnp.where(allowed, scores, -jnp.inf), axis=-1)), own)
    expos = jnp.where(allowed, jnp.exp(scores - highest[..., None]), 0.0)
    own_exp = jnp.exp(own - highest)
    denom = lax.optimization_barrier(jnp.sum(expos, axis=-1)) + own_exp
    numer = jnp.einsum('bgp,bpd->bgd', expos.astype(jnp.bfloat16).astype(jnp.float32), cached_values)
    numer = numer + own_exp.astype(jnp.bfloat16).astype(jnp.float32)[..., None] * own_pair[:, 1][:, None, :]
    return (numer / denom[..., None]).astype(jnp.bfloat16)

def reference(prefill_x, decode_x, query_weight, keyvalue_weight, key_cache, value_cache, cache_lengths, chain_order):
    order = chain_order.astype(jnp.int32)
    query_w = query_weight.reshape(N_REP, BLOCK_ROWS, HQ * HD)[order].reshape(D, HQ * HD)
    keyvalue_w = keyvalue_weight.reshape(N_REP, BLOCK_ROWS, 2 * KVH * HD)[order].reshape(D, 2 * KVH * HD)
    rows_all = jnp.concatenate([prefill_x, decode_x], axis=0)
    queries = jnp.dot(rows_all, query_w, preferred_element_type=jnp.float32).astype(jnp.bfloat16)
    keyvalues = jnp.dot(rows_all, keyvalue_w, preferred_element_type=jnp.float32).astype(jnp.bfloat16)
    pre_attention = prefill_attention(queries[:TOKENS], keyvalues[:TOKENS])
    query_all = queries[TOKENS:].reshape(BATCH, HQ, HD)
    new_all = keyvalues[TOKENS:].reshape(BATCH, KVH, 2, HD)
    lengths = cache_lengths.astype(jnp.int32)
    heads_out = lax.map(lambda index: decode_head(index, query_all, new_all, key_cache, value_cache, lengths), jnp.arange(KVH, dtype=jnp.int32))
    dec_attention = heads_out.transpose(1, 0, 2, 3).reshape(BATCH, HQ * HD)
    return (pre_attention, dec_attention)
```

```python
import functools
import math

import jax
import jax.numpy as jnp
import numpy as np
from jax import lax
from jax.experimental import pallas as pl
from jax.experimental.pallas import tpu as pltpu
from jax.sharding import Mesh
from jax.sharding import PartitionSpec as P

HD = 128
SEQ_LEN = 128
HEADS = 8
BATCH = 48
ROWS = 256
WIDTH = 1024
HALF = 640
SCALE = 1.0 / math.sqrt(HD)
REP = ("xl", "z", "c")
X = ("xl", "xh")
negative_big = -1e30
PER_STEP = 4


def flat_x(x):
    return (x % 2) * 2 + x // 2


def ring(value, axes, size, shift):
    pairs = [(i, (i + shift) % size) for i in range(size)]
    if axes == X:
        pairs = [(flat_x(i), flat_x(j)) for i, j in pairs]
    return lax.ppermute(value, axes, pairs)


def around(value, axes, cut):
    before = ring(value, axes, 4, 1)
    after = ring(value, axes, 4, -1)
    far_top = ring(before[:cut], axes, 4, 1)
    far_low = ring(after[cut:], axes, 4, -1)
    return jnp.concatenate([value, before, after, far_top, far_low], axis=0)


def slot_of(place, here):
    gap = (place - here) % 4
    return jnp.where(gap == 0, 0, jnp.where(gap == 3, 1, jnp.where(gap == 1, 2, 3)))


def project_kernel(col_ref, sy_ref, sp_ref, so_ref, sd_ref, xa_ref, xb_ref, w1_ref, w2_ref, out_ref, acc):
    step = pl.program_id(0)
    steps = pl.num_programs(0)

    @pl.when(step == 0)
    def _():
        acc[...] = jnp.zeros_like(acc)

    def add(w_ref):
        total = None
        for k in range(PER_STEP):
            j = step * PER_STEP + k
            cols = pl.ds(pl.multiple_of(col_ref[j] * 256, 256), 256)
            sy = sy_ref[j]
            sp = pl.ds(pl.multiple_of(sp_ref[j] * 128, 128), 128)
            so = pl.ds(pl.multiple_of(so_ref[j] * 128, 128), 128)
            sd = pl.ds(pl.multiple_of(512 + sd_ref[j] * 48, 16), 48)
            sy_rows = pl.ds(pl.multiple_of(sy * 128, 128), 128)
            lhs = jnp.concatenate(
                [
                    xa_ref[sy, sp, cols],
                    xb_ref[sp_ref[j], sy_rows, cols],
                    xa_ref[sy, sd, cols],
                    xa_ref[sy, so, cols],
                    xb_ref[so_ref[j], sy_rows, cols],
                ],
                axis=0,
            )
            part = jnp.dot(lhs, w_ref[k], preferred_element_type=jnp.float32)
            total = part if total is None else total + part
        acc[...] += total

    @pl.when(step < steps // 2)
    def _():
        add(w1_ref)

    @pl.when(step >= steps // 2)
    def _():
        add(w2_ref)

    @pl.when(step == steps - 1)
    def _():
        out_ref[...] = acc[...].astype(out_ref.dtype)


def project(tables, xa, xb, w1, w2):
    steps = 32 // PER_STEP
    half = steps // 2
    rows = 2 * ROWS + BATCH
    whole = lambda shape: pl.BlockSpec(shape, lambda s, *_: (0,) * len(shape), pipeline_mode=pl.Buffered(1))
    return pl.pallas_call(
        project_kernel,
        grid_spec=pltpu.PrefetchScalarGridSpec(
            num_scalar_prefetch=5,
            grid=(steps,),
            in_specs=[
                whole(xa.shape),
                whole(xb.shape),
                pl.BlockSpec((PER_STEP, ROWS, HALF), lambda s, *_: (jnp.minimum(s, half - 1), 0, 0)),
                pl.BlockSpec((PER_STEP, ROWS, HALF), lambda s, *_: (jnp.maximum(s - half, 0), 0, 0)),
            ],
            out_specs=pl.BlockSpec((rows, HALF), lambda s, *_: (0, 0)),
            scratch_shapes=[pltpu.VMEM((rows, HALF), jnp.float32)],
        ),
        out_shape=jax.ShapeDtypeStruct((rows, HALF), jnp.bfloat16),
        compiler_params=pltpu.CompilerParams(vmem_limit_bytes=48 * 1024 * 1024),
        cost_estimate=pl.CostEstimate(flops=2 * rows * 8192 * HALF, bytes_accessed=22_000_000, transcendentals=0),
        name="project",
    )(*tables, xa, xb, w1, w2)


def prefill_kernel(side_ref, mine_ref, other_ref, out_ref):
    first = side_ref[0] == 0
    mine, other = mine_ref[...], other_ref[...]
    low = jnp.where(first, mine, other)
    high = jnp.where(first, other, mine)
    keys, values = low[:, 512:], high[:, 512:]
    row = lax.broadcasted_iota(jnp.int32, (SEQ_LEN, SEQ_LEN), 0)
    col = lax.broadcasted_iota(jnp.int32, (SEQ_LEN, SEQ_LEN), 1)
    causal = row >= col
    for head in range(HEADS):
        part = low if head < 4 else high
        query = part[:, (head % 4) * HD : (head % 4 + 1) * HD]
        scores = lax.dot_general(query, keys, (((1,), (1,)), ((), ())), preferred_element_type=jnp.float32) * SCALE
        scores = jnp.where(causal, scores, negative_big)
        expos = jnp.exp(scores - jnp.max(scores, axis=-1, keepdims=True))
        sums = jnp.sum(expos, axis=-1, keepdims=True)
        weighted = jnp.dot(expos.astype(jnp.bfloat16), values, preferred_element_type=jnp.float32) / sums
        out_ref[:, head * HD : (head + 1) * HD] = weighted.astype(out_ref.dtype)


def prefill(side, mine, other):
    return pl.pallas_call(
        prefill_kernel,
        grid_spec=pltpu.PrefetchScalarGridSpec(
            num_scalar_prefetch=1,
            grid=(ROWS // SEQ_LEN,),
            in_specs=[pl.BlockSpec((SEQ_LEN, HALF), lambda s, *_: (s, 0))] * 2,
            out_specs=pl.BlockSpec((SEQ_LEN, WIDTH), lambda s, *_: (s, 0)),
        ),
        out_shape=jax.ShapeDtypeStruct((ROWS, WIDTH), jnp.bfloat16),
        cost_estimate=pl.CostEstimate(flops=70_000_000, bytes_accessed=1_200_000, transcendentals=262144),
        name="prefill_attention",
    )(side, mine, other)


def decode(side, mine, other, key_cache, value_cache, lengths, rep):
    low = jnp.where(side == 0, mine, other)
    high = jnp.where(side == 0, other, mine)
    queries = jnp.concatenate([low[:, :512].reshape(BATCH, 4, HD), high[:, :512].reshape(BATCH, 4, HD)], axis=1)
    own_key, own_value = low[:, 512:], high[:, 512:]
    positions_here = key_cache.shape[1]
    scores = jnp.einsum("bgd,bpd->bgp", queries, key_cache, preferred_element_type=jnp.float32) * SCALE
    position = rep * positions_here + jnp.arange(positions_here, dtype=jnp.int32)
    allowed = (position[None, :] < lengths[:, None])[:, None, :]
    own = jnp.einsum("bgd,bd->bg", queries, own_key, preferred_element_type=jnp.float32) * SCALE
    with_own = rep == 0
    own = jnp.where(with_own, own, negative_big)
    local_max = jnp.maximum(jnp.max(jnp.where(allowed, scores, negative_big), axis=-1), own)
    expos = jnp.where(allowed, jnp.exp(scores - local_max[..., None]), 0.0)
    own_exp = jnp.where(with_own, jnp.exp(own - local_max), 0.0)
    local_sum = jnp.sum(expos, axis=-1) + own_exp
    local_out = jnp.einsum(
        "bgp,bpd->bgd", expos.astype(jnp.bfloat16), value_cache, preferred_element_type=jnp.float32
    )
    local_out = local_out + own_exp.astype(jnp.bfloat16).astype(jnp.float32)[..., None] * own_value.astype(jnp.float32)[:, None, :]
    count = 32
    pairs = BATCH * HEADS // count
    stats = jnp.stack([local_max.reshape(count, pairs), local_sum.reshape(count, pairs)], axis=1)
    stats = jnp.pad(stats, ((0, 0), (0, 16 - pairs - 2), (0, HD - pairs)))
    packed = jnp.concatenate([local_out.reshape(count, pairs, HD), stats], axis=1)
    got = lax.all_to_all(packed, REP, 0, 0, tiled=True)
    tops, sums, outs = got[:, pairs, :pairs], got[:, pairs + 1, :pairs], got[:, :pairs]
    highest = jnp.max(tops, axis=0)
    keep = jnp.exp(tops - highest[None])
    numer = jnp.sum(outs * keep[:, :, None], axis=0)
    denom = jnp.sum(sums * keep, axis=0)
    done = jnp.pad((numer / denom[:, None]).astype(jnp.bfloat16), ((0, 16 - pairs), (0, 0)))
    every = lax.all_to_all(jnp.broadcast_to(done[None], (count, 16, HD)), REP, 0, 0, tiled=True)
    return every[:, :pairs].reshape(BATCH, HEADS * HD)


def per_device(prefill_x, decode_x, query_weight, keyvalue_weight, key_cache, value_cache, cache_lengths, chain_order):
    xl, z, c = lax.axis_index("xl"), lax.axis_index("z"), lax.axis_index("c")
    xh, y = lax.axis_index("xh"), lax.axis_index("y")
    x = xh * 2 + xl
    rep = xl * 16 + z * 2 + c

    first = jnp.concatenate([query_weight[:, :512], keyvalue_weight[:, :HD]], axis=1)
    second = jnp.concatenate([query_weight[:, 512:], keyvalue_weight[:, HD:]], axis=1)
    kept = jnp.where(xl == 0, first, second)
    given = jnp.where(xl == 0, second, first)
    w1 = lax.all_gather(kept, ("z", "c"))
    w2 = lax.all_gather(ring(given, "xl", 2, 1), ("z", "c"))

    top, low = prefill_x[:128], prefill_x[128:]
    decode_other = lax.ppermute(decode_x, X, [(flat_x(i), flat_x(3 - i)) for i in range(4)])
    xa = around(top, X, 64)
    xb = around(low, "y", 64)
    xa = around(jnp.concatenate([xa, decode_x, decode_other], axis=0), "y", 304).reshape(4, 608, WIDTH)
    xb = around(xb, X, 256).reshape(4, 512, WIDTH)

    near = xl * 16 + jnp.arange(16, dtype=jnp.int32)
    stored = jnp.concatenate([near, (near + 16) % 32])
    logical = jnp.sum(
        jnp.where(chain_order[None, :] == stored[:, None], jnp.arange(32, dtype=jnp.int32)[None, :], 0), axis=1
    )
    group = logical // 4
    from_xh, from_y = group // 4, group % 4
    tables = (
        logical % 4,
        slot_of(from_y, y),
        slot_of(2 * from_xh + 1 - xl, x),
        slot_of(2 * from_xh + xl, x),
        (from_xh != xh).astype(jnp.int32),
    )
    rows = project(tables, xa, xb, w1, w2)
    dec_mine = rows[ROWS : ROWS + BATCH]
    pre_mine = rows[ROWS + BATCH :]
    dec_other = ring(dec_mine, "xl", 2, 1)
    pre_other = ring(rows[:ROWS], "xl", 2, 1)
    attn_dec = decode(xl, dec_mine, dec_other, key_cache, value_cache, cache_lengths, rep)
    attn_pre = prefill(xl.reshape(1).astype(jnp.int32), pre_mine, pre_other)
    return attn_pre, attn_dec


def solution(mesh):
    fine = Mesh(np.asarray(mesh.devices).reshape(2, 8, 2, 2, 4), ("xl", "z", "c", "xh", "y"))
    rep, tp = REP, ("xh", "y")
    in_specs = (P(rep, tp), P(None, tp), P(rep, tp), P(rep, tp), P(None, rep, tp), P(None, rep, tp), P(), P())
    out_specs = (P(rep, tp), P(None, tp))
    return jax.shard_map(per_device, mesh=fine, in_specs=in_specs, out_specs=out_specs, check_vma=False)
```

```python
import functools
import math

import jax
import jax.numpy as jnp
import numpy as np
from jax import lax
from jax.experimental import pallas as pl
from jax.experimental.pallas import tpu as pltpu
from jax.sharding import Mesh
from jax.sharding import PartitionSpec as P

HD = 128
SEQ_LEN = 128
HEADS = 8
BATCH = 48
ROWS = 256
WIDTH = 1024
HALF = 640
COUNT = 32
SCALE = 1.0 / math.sqrt(HD)
REP = ("xl", "z", "c")
X = ("xl", "xh")
STEPS = (0, 3, 1, 2)
OWN, PARTNER = (0, 3), (1, 2)
negative_big = -1e30
f32 = jnp.float32


def flat_x(x):
    return (x % 2) * 2 + x // 2


def ring(value, axes, size, shift):
    pairs = [(i, (i + shift) % size) for i in range(size)]
    if axes == X:
        pairs = [(flat_x(i), flat_x(j)) for i, j in pairs]
    return lax.ppermute(value, axes, pairs)


def around(value, axes):
    return [value, ring(value, axes, 4, 1), ring(value, axes, 4, -1), ring(value, axes, 4, 2)]


def vmem(count):
    return [pl.BlockSpec(memory_space=pltpu.VMEM)] * count


def smem(count):
    return [pl.BlockSpec(memory_space=pltpu.SMEM)] * count


def anywhere(count):
    return [pl.BlockSpec(memory_space=pl.ANY)] * count


def params(mebibytes=12):
    return pltpu.CompilerParams(vmem_limit_bytes=mebibytes * 1024 * 1024)


def shaped(dtype, *shape):
    return jax.ShapeDtypeStruct(shape, dtype)


bf16 = functools.partial(shaped, jnp.bfloat16)


def split_kernel(place_ref, qw_ref, kv_ref, kept_ref, given_ref, sems):
    def write(left_ref, right_ref):
        copies = [
            pltpu.make_async_copy(qw_ref.at[:, :512], left_ref.at[:, :512], sems.at[0]),
            pltpu.make_async_copy(kv_ref.at[:, :HD], left_ref.at[:, 512:], sems.at[1]),
            pltpu.make_async_copy(qw_ref.at[:, 512:], right_ref.at[:, :512], sems.at[2]),
            pltpu.make_async_copy(kv_ref.at[:, HD:], right_ref.at[:, 512:], sems.at[3]),
        ]
        for copy in copies:
            copy.start()
        for copy in copies:
            copy.wait()

    @pl.when(place_ref[0] == 0)
    def _():
        write(kept_ref, given_ref)

    @pl.when(place_ref[0] != 0)
    def _():
        write(given_ref, kept_ref)


def split(place, qw, kv):
    return pl.pallas_call(
        split_kernel,
        in_specs=smem(1) + anywhere(2),
        out_specs=anywhere(2),
        out_shape=[bf16(ROWS, HALF)] * 2,
        scratch_shapes=[pltpu.SemaphoreType.DMA((4,))],
        compiler_params=params(),
        name="split",
    )(place, qw, kv)


def pack_kernel(*refs):
    row = 0
    for ref in refs[:-1]:
        refs[-1][row : row + ref.shape[0]] = ref[...]
        row += ref.shape[0]


def pack(parts):
    return pl.pallas_call(
        pack_kernel,
        in_specs=vmem(len(parts)),
        out_specs=pl.BlockSpec(memory_space=pltpu.VMEM),
        out_shape=bf16(sum(v.shape[0] for v in parts), parts[0].shape[1]),
        compiler_params=params(),
        name="pack",
    )(*parts)


def project_kernel(place_ref, logical_ref, *refs):
    a_refs, b_refs, w_ref, theirs_ref, mine_ref = refs[:4], refs[4:8], refs[8], refs[9], refs[10]
    x_all, w_all, acc, x_sem, w_sem = refs[11:]
    x, y = place_ref[1], place_ref[2]
    moves = []
    for i in range(4):
        for k in range(4):
            base = ROWS if k in OWN else 0
            group = (((x + STEPS[k]) % 4) // 2) * 4 + (y + STEPS[i]) % 4
            moves.append((a_refs[i].at[k * 128 : (k + 1) * 128], x_all.at[group, base : base + 128]))
            base = (ROWS if i in OWN else 0) + 128
            group = (((x + STEPS[i]) % 4) // 2) * 4 + (y + STEPS[k]) % 4
            moves.append((b_refs[i].at[k * 128 : (k + 1) * 128], x_all.at[group, base : base + 128]))
    moves = [pltpu.make_async_copy(src, dst, x_sem.at[n]) for n, (src, dst) in enumerate(moves)]
    loads = [pltpu.make_async_copy(w_ref.at[i], w_all.at[i], w_sem.at[i]) for i in range(8)]
    for copy in moves + loads:
        copy.start()
    for copy in moves:
        copy.wait()
    for i in range(8):
        loads[i].wait()
        lhs = []
        for k in range(4):
            block = logical_ref[4 * i + k]
            lhs.append(x_all[block // 4, :, pl.ds(pl.multiple_of((block % 4) * ROWS, ROWS), ROWS)])
        part = jnp.dot(jnp.concatenate(lhs, axis=1), w_all[i], preferred_element_type=f32)
        if i == 0:
            acc[...] = part
        elif i < 7:
            acc[...] += part
        else:
            done = (acc[...] + part).astype(jnp.bfloat16)
            theirs_ref[...] = done[:ROWS]
            mine_ref[...] = done[ROWS:]


def project(place, logical, a, b, w):
    rows = 2 * ROWS
    return pl.pallas_call(
        project_kernel,
        in_specs=smem(2) + anywhere(9),
        out_specs=vmem(2),
        out_shape=[bf16(ROWS, HALF)] * 2,
        scratch_shapes=[
            pltpu.VMEM((8, rows, WIDTH), jnp.bfloat16),
            pltpu.VMEM((8, 4 * ROWS, HALF), jnp.bfloat16),
            pltpu.VMEM((rows, HALF), f32),
            pltpu.SemaphoreType.DMA((32,)),
            pltpu.SemaphoreType.DMA((8,)),
        ],
        compiler_params=params(48),
        cost_estimate=pl.CostEstimate(flops=2 * rows * 8192 * HALF, bytes_accessed=19_000_000, transcendentals=0),
        name="project",
    )(place, logical, *a, *b, w)


def prefill_kernel(place_ref, mine_ref, other_ref, out_ref):
    first = place_ref[0] == 0
    mine, other = mine_ref[...], other_ref[...]
    low = jnp.where(first, mine, other)
    high = jnp.where(first, other, mine)
    row = lax.broadcasted_iota(jnp.int32, (SEQ_LEN, SEQ_LEN), 0)
    col = lax.broadcasted_iota(jnp.int32, (SEQ_LEN, SEQ_LEN), 1)
    causal = row >= col
    causal = jnp.concatenate([causal] * HEADS, axis=0)
    for n in range(ROWS // SEQ_LEN):
        at = slice(n * SEQ_LEN, (n + 1) * SEQ_LEN)
        keys, values = low[at, 512:], high[at, 512:]
        queries = [part[at, h * HD : (h + 1) * HD] for part in (low, high) for h in range(4)]
        scores = lax.dot_general(
            jnp.concatenate(queries, axis=0), keys, (((1,), (1,)), ((), ())), preferred_element_type=f32
        ) * SCALE
        scores = jnp.where(causal, scores, negative_big)
        expos = jnp.exp(scores - jnp.max(scores, axis=-1, keepdims=True))
        sums = jnp.sum(expos, axis=-1, keepdims=True)
        weighted = (jnp.dot(expos.astype(jnp.bfloat16), values, preferred_element_type=f32) / sums).astype(jnp.bfloat16)
        for head in range(HEADS):
            out_ref[at, head * HD : (head + 1) * HD] = weighted[head * SEQ_LEN : (head + 1) * SEQ_LEN]


def prefill(place, mine, other):
    return pl.pallas_call(
        prefill_kernel,
        in_specs=smem(1) + vmem(2),
        out_specs=pl.BlockSpec(memory_space=pltpu.VMEM),
        out_shape=bf16(ROWS, WIDTH),
        compiler_params=params(),
        cost_estimate=pl.CostEstimate(flops=140_000_000, bytes_accessed=1_200_000, transcendentals=262144),
        name="prefill_attention",
    )(place, mine, other)


def partial_kernel(x_ref, qw_ref, kv_ref, out_ref):
    x = x_ref[...]
    for col, part in ((0, jnp.dot(x, qw_ref[...], preferred_element_type=f32)), (8, jnp.dot(x, kv_ref[...], preferred_element_type=f32))):
        for i in range(BATCH // 8):
            for j in range(part.shape[1] // HD):
                out_ref[i * 10 + col + j] = part[i * 8 : (i + 1) * 8, j * HD : (j + 1) * HD]
    out_ref[60:] = jnp.zeros((4, 8, HD), f32)


def partial(x, qw, kv):
    return pl.pallas_call(
        partial_kernel,
        in_specs=vmem(3),
        out_specs=pl.BlockSpec(memory_space=pltpu.VMEM),
        out_shape=shaped(f32, 64, 8, HD),
        compiler_params=params(),
        name="decode_partial",
    )(x, qw, kv)


def total_kernel(in_ref, out_ref):
    both = [jnp.sum(in_ref[:, m], axis=0) for m in range(2)]
    done = jnp.concatenate(both, axis=0).astype(jnp.bfloat16)
    out_ref[...] = jnp.broadcast_to(done[None], out_ref.shape)


def total(shares):
    return pl.pallas_call(
        total_kernel,
        in_specs=vmem(1),
        out_specs=pl.BlockSpec(memory_space=pltpu.VMEM),
        out_shape=bf16(COUNT, 16, HD),
        compiler_params=params(),
        name="decode_total",
    )(shares.reshape(COUNT, 2, 8, HD))


def decode_kernel(place_ref, length_ref, tile_ref, key_hbm, value_hbm, out_ref, rows_ref, score_ref, length_rows, key_ref, value_ref, sems):
    loads = [pltpu.make_async_copy(key_hbm, key_ref, sems.at[0]), pltpu.make_async_copy(value_hbm, value_ref, sems.at[1])]
    for load in loads:
        load.start()
    rep = place_ref[3]
    with_own = rep == 0
    for i in range(BATCH // 8):
        for j in range(10):
            t = i * 10 + j
            tile = tile_ref[t // 2, (t % 2) * 8 : (t % 2 + 1) * 8, :].astype(f32)
            rows_ref[i * 8 : (i + 1) * 8, j, :] = tile
    loads[0].wait()
    for b in range(BATCH):
        score_ref[b] = lax.dot_general(
            rows_ref[b, 0:8].astype(jnp.bfloat16), key_ref[b], (((1,), (1,)), ((), ())), preferred_element_type=f32
        )
        length_rows[b] = jnp.full((8, HD), length_ref[b], jnp.int32)
    lane = lax.broadcasted_iota(jnp.int32, (8, HD), 1)
    position = (rep * key_ref.shape[1] + lane)[None]
    loads[1].wait()
    for i in range(BATCH // 8):
        at = slice(i * 8, (i + 1) * 8)
        scores = score_ref[at] * SCALE
        own = jnp.sum(rows_ref[at, 0:8] * rows_ref[at, 8:9], axis=-1, keepdims=True) * SCALE
        allowed = position < length_rows[at]
        own = jnp.where(with_own, own, negative_big)
        top = jnp.maximum(jnp.max(jnp.where(allowed, scores, negative_big), axis=-1, keepdims=True), own)
        expos = jnp.where(allowed, jnp.exp(scores - top), 0.0)
        own_exp = jnp.where(with_own, jnp.exp(own - top), 0.0)
        sums = jnp.sum(expos, axis=-1, keepdims=True) + own_exp
        extra = own_exp.astype(jnp.bfloat16).astype(f32) * rows_ref[at, 9:10]
        weights = expos.astype(jnp.bfloat16)
        for k in range(0, 8, 2):
            pair = (i * 8 + k) // 2
            for m in range(2):
                outs = jnp.dot(weights[k + m], value_ref[i * 8 + k + m], preferred_element_type=f32)
                out_ref[pair, 8 * m : 8 * (m + 1)] = outs + extra[k + m]
            stats = jnp.where(lane == 0, top[k], jnp.where(lane == 1, sums[k], 1.0))
            out_ref[pair, 16:24] = jnp.where(lane == 2, top[k + 1], jnp.where(lane == 3, sums[k + 1], stats))
    out_ref[BATCH // 2 :] = jnp.ones((COUNT - BATCH // 2, 24, HD), f32)


def decode(place, lengths, tiles, keys, values):
    return pl.pallas_call(
        decode_kernel,
        in_specs=smem(2) + vmem(1) + anywhere(2),
        out_specs=pl.BlockSpec(memory_space=pltpu.VMEM),
        out_shape=shaped(f32, COUNT, 24, HD),
        scratch_shapes=[
            pltpu.VMEM((BATCH, 16, HD), f32),
            pltpu.VMEM((BATCH, 8, HD), f32),
            pltpu.VMEM((BATCH, 8, HD), jnp.int32),
            pltpu.VMEM((BATCH, HD, HD), jnp.bfloat16),
            pltpu.VMEM((BATCH, HD, HD), jnp.bfloat16),
            pltpu.SemaphoreType.DMA((2,)),
        ],
        compiler_params=params(),
        cost_estimate=pl.CostEstimate(flops=30_000_000, bytes_accessed=4_000_000, transcendentals=50000),
        name="decode_attention",
    )(place, lengths, tiles, keys, values)


def combine_kernel(in_ref, out_ref):
    stats = in_ref[:, 16:24]
    done = []
    for m in range(2):
        tops, sums = stats[:, :, 2 * m : 2 * m + 1], stats[:, :, 2 * m + 1 : 2 * m + 2]
        keep = jnp.exp(tops - jnp.max(tops, axis=0, keepdims=True))
        numer = jnp.sum(in_ref[:, 8 * m : 8 * (m + 1)] * keep, axis=0)
        done.append(numer / jnp.sum(sums * keep, axis=0))
    done = jnp.concatenate(done, axis=0).astype(jnp.bfloat16)
    out_ref[...] = jnp.broadcast_to(done[None], out_ref.shape)


def combine(parts):
    return pl.pallas_call(
        combine_kernel,
        in_specs=vmem(1),
        out_specs=pl.BlockSpec(memory_space=pltpu.VMEM),
        out_shape=bf16(COUNT, 16, HD),
        compiler_params=params(),
        name="decode_combine",
    )(parts)


def swap_all(value):
    return lax.all_to_all(value, REP, 0, 0, tiled=True)


def per_device(prefill_x, decode_x, query_weight, keyvalue_weight, key_cache, value_cache, cache_lengths, chain_order):
    xl, z, c = lax.axis_index("xl"), lax.axis_index("z"), lax.axis_index("c")
    xh, y = lax.axis_index("xh"), lax.axis_index("y")
    x = xh * 2 + xl
    rep = xl * 16 + z * 2 + c
    place = jnp.stack([xl, x, y, rep]).astype(jnp.int32)
    blocks = jnp.arange(COUNT, dtype=jnp.int32)

    barrier = lax.optimization_barrier
    block = jnp.sum(jnp.where(chain_order == rep, blocks, 0))
    piece_x = lax.dynamic_slice(decode_x, (0, (block % 4) * ROWS), (BATCH, ROWS))
    piece_x = jnp.where(block // 4 == xh * 4 + y, piece_x, jnp.zeros_like(piece_x))

    kept, given = split(place, query_weight, keyvalue_weight)
    got = ring(given, "xl", 2, 1)
    xb = around(prefill_x[128:], "y")
    piece_x = piece_x + ring(piece_x, "xh", 2, 1)
    got, piece_x, xb[1], xb[2] = barrier((got, piece_x, xb[1], xb[2]))
    weights = lax.all_gather(jnp.stack([kept, got]), ("z", "c"))

    piece_x = piece_x + ring(piece_x, "y", 4, 1) + ring(piece_x, "y", 4, -1) + ring(piece_x, "y", 4, 2)
    xa = around(prefill_x[:128], X)
    shares = partial(piece_x, query_weight, keyvalue_weight)
    shares, *xs = barrier((shares, *xa, *xb))
    shares = swap_all(shares)

    xa, xb = pack(xs[:4]), pack(xs[4:])
    xa, xb = around(xa, "y"), [xb, ring(xb, X, 4, 1), ring(xb, X, 4, -1)]
    shares, xb[1], xb[2] = barrier((shares, xb[1], xb[2]))
    tiles = total(shares)
    tiles, opposite = barrier((tiles, xb[0]))
    xb.append(ring(opposite, X, 4, 2))
    tiles = swap_all(tiles)
    parts = swap_all(decode(place, cache_lengths, tiles, key_cache, value_cache))

    near = jnp.arange(16, dtype=jnp.int32)
    stored = jnp.stack([xl * 16 + near, (1 - xl) * 16 + near], axis=1).reshape(COUNT)
    logical = jnp.sum(jnp.where(chain_order[None, :] == stored[:, None], blocks[None, :], 0), axis=1)
    theirs, mine = project(place, logical, xa, xb, weights.reshape(8, 4 * ROWS, HALF))
    theirs, parts = barrier((theirs, parts))
    other = ring(theirs, "xl", 2, 1)
    attn_dec = swap_all(combine(parts))[: BATCH // 2].reshape(BATCH, WIDTH)
    attn_pre = prefill(place, mine, other)
    return attn_pre, attn_dec


def solution(mesh):
    fine = Mesh(np.asarray(mesh.devices).reshape(2, 8, 2, 2, 4), ("xl", "z", "c", "xh", "y"))
    rep, tp = REP, ("xh", "y")
    in_specs = (P(rep, tp), P(None, tp), P(rep, tp), P(rep, tp), P(None, rep, tp), P(None, rep, tp), P(), P())
    out_specs = (P(rep, tp), P(None, tp))
    return jax.shard_map(per_device, mesh=fine, in_specs=in_specs, out_specs=out_specs, check_vma=False)
```

```python
import functools
import math

import jax
import jax.numpy as jnp
import numpy as np
from jax import lax
from jax.experimental import pallas as pl
from jax.experimental.pallas import tpu as pltpu
from jax.sharding import Mesh
from jax.sharding import PartitionSpec as P

HD = 128
SEQ_LEN = 128
HEADS = 8
BATCH = 48
ROWS = 256
WIDTH = 1024
HALF = 640
COUNT = 32
SCALE = 1.0 / math.sqrt(HD)
REP = ("xl", "z", "c")
X = ("xl", "xh")
STEPS = (0, 3, 1, 2)
OWN, PARTNER = (0, 3), (1, 2)
negative_big = -1e30
f32 = jnp.float32


def flat_x(x):
    return (x % 2) * 2 + x // 2


def ring(value, axes, size, shift):
    pairs = [(i, (i + shift) % size) for i in range(size)]
    if axes == X:
        pairs = [(flat_x(i), flat_x(j)) for i, j in pairs]
    return lax.ppermute(value, axes, pairs)


def around(value, axes):
    return [value, ring(value, axes, 4, 1), ring(value, axes, 4, -1), ring(value, axes, 4, 2)]


def vmem(count):
    return [pl.BlockSpec(memory_space=pltpu.VMEM)] * count


def smem(count):
    return [pl.BlockSpec(memory_space=pltpu.SMEM)] * count


def anywhere(count):
    return [pl.BlockSpec(memory_space=pl.ANY)] * count


def params(mebibytes=12):
    return pltpu.CompilerParams(vmem_limit_bytes=mebibytes * 1024 * 1024)


def shaped(dtype, *shape):
    return jax.ShapeDtypeStruct(shape, dtype)


bf16 = functools.partial(shaped, jnp.bfloat16)


def split_kernel(place_ref, qw_ref, kv_ref, kept_ref, given_ref, sems):
    def write(left_ref, right_ref):
        copies = [
            pltpu.make_async_copy(qw_ref.at[:, :512], left_ref.at[:, :512], sems.at[0]),
            pltpu.make_async_copy(kv_ref.at[:, :HD], left_ref.at[:, 512:], sems.at[1]),
            pltpu.make_async_copy(qw_ref.at[:, 512:], right_ref.at[:, :512], sems.at[2]),
            pltpu.make_async_copy(kv_ref.at[:, HD:], right_ref.at[:, 512:], sems.at[3]),
        ]
        for copy in copies:
            copy.start()
        for copy in copies:
            copy.wait()

    @pl.when(place_ref[0] == 0)
    def _():
        write(kept_ref, given_ref)

    @pl.when(place_ref[0] != 0)
    def _():
        write(given_ref, kept_ref)


def split(place, qw, kv):
    return pl.pallas_call(
        split_kernel,
        in_specs=smem(1) + anywhere(2),
        out_specs=anywhere(2),
        out_shape=[bf16(ROWS, HALF)] * 2,
        scratch_shapes=[pltpu.SemaphoreType.DMA((4,))],
        compiler_params=params(),
        name="split",
    )(place, qw, kv)


def pack_kernel(*refs):
    row = 0
    for ref in refs[:-1]:
        refs[-1][row : row + ref.shape[0]] = ref[...]
        row += ref.shape[0]


def pack(parts):
    return pl.pallas_call(
        pack_kernel,
        in_specs=vmem(len(parts)),
        out_specs=pl.BlockSpec(memory_space=pltpu.VMEM),
        out_shape=bf16(sum(v.shape[0] for v in parts), parts[0].shape[1]),
        compiler_params=params(),
        name="pack",
    )(*parts)


def project_kernel(slots, place_ref, logical_ref, *refs):
    a_refs, b_refs, w_ref, out_ref = refs[:4], refs[4:8], refs[8], refs[9]
    x_all, w_all, acc, x_sem, w_sem = refs[10:]
    x, y = place_ref[1], place_ref[2]
    copies = []
    for n, slot in enumerate(slots):
        at_x = (x + STEPS[slot]) % 4
        for i in range(4):
            at_y = (y + STEPS[i]) % 4
            group = (at_x // 2) * 4 + at_y
            copies.append((a_refs[i].at[slot * 128 : (slot + 1) * 128], x_all.at[group, :128], 2 * (4 * n + i)))
            copies.append((b_refs[slot].at[i * 128 : (i + 1) * 128], x_all.at[group, 128:], 2 * (4 * n + i) + 1))
    copies = [pltpu.make_async_copy(src, dst, x_sem.at[s]) for src, dst, s in copies]
    loads = [pltpu.make_async_copy(w_ref.at[i], w_all.at[i], w_sem.at[i]) for i in range(8)]
    for copy in copies + loads:
        copy.start()
    for copy in copies:
        copy.wait()
    for i in range(8):
        loads[i].wait()
        lhs = []
        for k in range(4):
            block = logical_ref[4 * i + k]
            lhs.append(x_all[block // 4, :, pl.ds(pl.multiple_of((block % 4) * ROWS, ROWS), ROWS)])
        part = jnp.dot(jnp.concatenate(lhs, axis=1), w_all[i], preferred_element_type=f32)
        if i == 0:
            acc[...] = part
        elif i < 7:
            acc[...] += part
        else:
            out_ref[...] = (acc[...] + part).astype(out_ref.dtype)


def project(slots, place, logical, a, b, w):
    return pl.pallas_call(
        functools.partial(project_kernel, slots),
        in_specs=smem(2) + anywhere(9),
        out_specs=pl.BlockSpec(memory_space=pltpu.VMEM),
        out_shape=bf16(ROWS, HALF),
        scratch_shapes=[
            pltpu.VMEM((8, ROWS, WIDTH), jnp.bfloat16),
            pltpu.VMEM((8, 4 * ROWS, HALF), jnp.bfloat16),
            pltpu.VMEM((ROWS, HALF), f32),
            pltpu.SemaphoreType.DMA((16,)),
            pltpu.SemaphoreType.DMA((8,)),
        ],
        compiler_params=params(48),
        cost_estimate=pl.CostEstimate(flops=2 * ROWS * 8192 * HALF, bytes_accessed=15_000_000, transcendentals=0),
        name="project",
    )(place, logical, *a, *b, w)


def prefill_kernel(place_ref, mine_ref, other_ref, out_ref):
    first = place_ref[0] == 0
    mine, other = mine_ref[...], other_ref[...]
    low = jnp.where(first, mine, other)
    high = jnp.where(first, other, mine)
    row = lax.broadcasted_iota(jnp.int32, (SEQ_LEN, SEQ_LEN), 0)
    col = lax.broadcasted_iota(jnp.int32, (SEQ_LEN, SEQ_LEN), 1)
    causal = row >= col
    causal = jnp.concatenate([causal] * HEADS, axis=0)
    for n in range(ROWS // SEQ_LEN):
        at = slice(n * SEQ_LEN, (n + 1) * SEQ_LEN)
        keys, values = low[at, 512:], high[at, 512:]
        queries = [part[at, h * HD : (h + 1) * HD] for part in (low, high) for h in range(4)]
        scores = lax.dot_general(
            jnp.concatenate(queries, axis=0), keys, (((1,), (1,)), ((), ())), preferred_element_type=f32
        ) * SCALE
        scores = jnp.where(causal, scores, negative_big)
        expos = jnp.exp(scores - jnp.max(scores, axis=-1, keepdims=True))
        sums = jnp.sum(expos, axis=-1, keepdims=True)
        weighted = (jnp.dot(expos.astype(jnp.bfloat16), values, preferred_element_type=f32) / sums).astype(jnp.bfloat16)
        for head in range(HEADS):
            out_ref[at, head * HD : (head + 1) * HD] = weighted[head * SEQ_LEN : (head + 1) * SEQ_LEN]


def prefill(place, mine, other):
    return pl.pallas_call(
        prefill_kernel,
        in_specs=smem(1) + vmem(2),
        out_specs=pl.BlockSpec(memory_space=pltpu.VMEM),
        out_shape=bf16(ROWS, WIDTH),
        compiler_params=params(),
        cost_estimate=pl.CostEstimate(flops=140_000_000, bytes_accessed=1_200_000, transcendentals=262144),
        name="prefill_attention",
    )(place, mine, other)


def partial_kernel(x_ref, qw_ref, kv_ref, out_ref):
    x = x_ref[...]
    for col, part in ((0, jnp.dot(x, qw_ref[...], preferred_element_type=f32)), (8, jnp.dot(x, kv_ref[...], preferred_element_type=f32))):
        for i in range(BATCH // 8):
            for j in range(part.shape[1] // HD):
                out_ref[i * 10 + col + j] = part[i * 8 : (i + 1) * 8, j * HD : (j + 1) * HD]
    out_ref[60:] = jnp.zeros((4, 8, HD), f32)


def partial(x, qw, kv):
    return pl.pallas_call(
        partial_kernel,
        in_specs=vmem(3),
        out_specs=pl.BlockSpec(memory_space=pltpu.VMEM),
        out_shape=shaped(f32, 64, 8, HD),
        compiler_params=params(),
        name="decode_partial",
    )(x, qw, kv)


def total_kernel(in_ref, out_ref):
    both = [jnp.sum(in_ref[:, m], axis=0) for m in range(2)]
    done = jnp.concatenate(both, axis=0).astype(jnp.bfloat16)
    out_ref[...] = jnp.broadcast_to(done[None], out_ref.shape)


def total(shares):
    return pl.pallas_call(
        total_kernel,
        in_specs=vmem(1),
        out_specs=pl.BlockSpec(memory_space=pltpu.VMEM),
        out_shape=bf16(COUNT, 16, HD),
        compiler_params=params(),
        name="decode_total",
    )(shares.reshape(COUNT, 2, 8, HD))


def decode_kernel(place_ref, length_ref, tile_ref, key_hbm, value_hbm, out_ref, rows_ref, score_ref, length_rows, key_ref, value_ref, sems):
    loads = [pltpu.make_async_copy(key_hbm, key_ref, sems.at[0]), pltpu.make_async_copy(value_hbm, value_ref, sems.at[1])]
    for load in loads:
        load.start()
    rep = place_ref[3]
    with_own = rep == 0
    for i in range(BATCH // 8):
        for j in range(10):
            t = i * 10 + j
            tile = tile_ref[t // 2, (t % 2) * 8 : (t % 2 + 1) * 8, :].astype(f32)
            rows_ref[i * 8 : (i + 1) * 8, j, :] = tile
    loads[0].wait()
    for b in range(BATCH):
        score_ref[b] = lax.dot_general(
            rows_ref[b, 0:8].astype(jnp.bfloat16), key_ref[b], (((1,), (1,)), ((), ())), preferred_element_type=f32
        )
        length_rows[b] = jnp.full((8, HD), length_ref[b], jnp.int32)
    lane = lax.broadcasted_iota(jnp.int32, (8, HD), 1)
    position = (rep * key_ref.shape[1] + lane)[None]
    loads[1].wait()
    for i in range(BATCH // 8):
        at = slice(i * 8, (i + 1) * 8)
        scores = score_ref[at] * SCALE
        own = jnp.sum(rows_ref[at, 0:8] * rows_ref[at, 8:9], axis=-1, keepdims=True) * SCALE
        allowed = position < length_rows[at]
        own = jnp.where(with_own, own, negative_big)
        top = jnp.maximum(jnp.max(jnp.where(allowed, scores, negative_big), axis=-1, keepdims=True), own)
        expos = jnp.where(allowed, jnp.exp(scores - top), 0.0)
        own_exp = jnp.where(with_own, jnp.exp(own - top), 0.0)
        sums = jnp.sum(expos, axis=-1, keepdims=True) + own_exp
        extra = own_exp.astype(jnp.bfloat16).astype(f32) * rows_ref[at, 9:10]
        weights = expos.astype(jnp.bfloat16)
        for k in range(0, 8, 2):
            pair = (i * 8 + k) // 2
            for m in range(2):
                outs = jnp.dot(weights[k + m], value_ref[i * 8 + k + m], preferred_element_type=f32)
                out_ref[pair, 8 * m : 8 * (m + 1)] = outs + extra[k + m]
            stats = jnp.where(lane == 0, top[k], jnp.where(lane == 1, sums[k], 1.0))
            out_ref[pair, 16:24] = jnp.where(lane == 2, top[k + 1], jnp.where(lane == 3, sums[k + 1], stats))
    out_ref[BATCH // 2 :] = jnp.ones((COUNT - BATCH // 2, 24, HD), f32)


def decode(place, lengths, tiles, keys, values):
    return pl.pallas_call(
        decode_kernel,
        in_specs=smem(2) + vmem(1) + anywhere(2),
        out_specs=pl.BlockSpec(memory_space=pltpu.VMEM),
        out_shape=shaped(f32, COUNT, 24, HD),
        scratch_shapes=[
            pltpu.VMEM((BATCH, 16, HD), f32),
            pltpu.VMEM((BATCH, 8, HD), f32),
            pltpu.VMEM((BATCH, 8, HD), jnp.int32),
            pltpu.VMEM((BATCH, HD, HD), jnp.bfloat16),
            pltpu.VMEM((BATCH, HD, HD), jnp.bfloat16),
            pltpu.SemaphoreType.DMA((2,)),
        ],
        compiler_params=params(56),
        cost_estimate=pl.CostEstimate(flops=30_000_000, bytes_accessed=4_000_000, transcendentals=50000),
        name="decode_attention",
    )(place, lengths, tiles, keys, values)


def combine_kernel(in_ref, out_ref):
    stats = in_ref[:, 16:24]
    done = []
    for m in range(2):
        tops, sums = stats[:, :, 2 * m : 2 * m + 1], stats[:, :, 2 * m + 1 : 2 * m + 2]
        keep = jnp.exp(tops - jnp.max(tops, axis=0, keepdims=True))
        numer = jnp.sum(in_ref[:, 8 * m : 8 * (m + 1)] * keep, axis=0)
        done.append(numer / jnp.sum(sums * keep, axis=0))
    done = jnp.concatenate(done, axis=0).astype(jnp.bfloat16)
    out_ref[...] = jnp.broadcast_to(done[None], out_ref.shape)


def combine(parts):
    return pl.pallas_call(
        combine_kernel,
        in_specs=vmem(1),
        out_specs=pl.BlockSpec(memory_space=pltpu.VMEM),
        out_shape=bf16(COUNT, 16, HD),
        compiler_params=params(),
        name="decode_combine",
    )(parts)


def swap_all(value):
    return lax.all_to_all(value, REP, 0, 0, tiled=True)


def per_device(prefill_x, decode_x, query_weight, keyvalue_weight, key_cache, value_cache, cache_lengths, chain_order):
    xl, z, c = lax.axis_index("xl"), lax.axis_index("z"), lax.axis_index("c")
    xh, y = lax.axis_index("xh"), lax.axis_index("y")
    x = xh * 2 + xl
    rep = xl * 16 + z * 2 + c
    place = jnp.stack([xl, x, y, rep]).astype(jnp.int32)
    blocks = jnp.arange(COUNT, dtype=jnp.int32)

    barrier = lax.optimization_barrier
    block = jnp.sum(jnp.where(chain_order == rep, blocks, 0))
    piece_x = lax.dynamic_slice(decode_x, (0, (block % 4) * ROWS), (BATCH, ROWS))
    piece_x = jnp.where(block // 4 == xh * 4 + y, piece_x, jnp.zeros_like(piece_x))

    kept, given = split(place, query_weight, keyvalue_weight)
    got = ring(given, "xl", 2, 1)
    xb = around(prefill_x[128:], "y")
    piece_x = piece_x + ring(piece_x, "xh", 2, 1)
    got, piece_x, xb[1], xb[2] = barrier((got, piece_x, xb[1], xb[2]))
    weights = lax.all_gather(jnp.stack([kept, got]), ("z", "c"))

    piece_x = piece_x + ring(piece_x, "y", 4, 1) + ring(piece_x, "y", 4, -1) + ring(piece_x, "y", 4, 2)
    xa = around(prefill_x[:128], X)
    shares = partial(piece_x, query_weight, keyvalue_weight)
    shares, *xs = barrier((shares, *xa, *xb))
    shares = swap_all(shares)

    xa, xb = pack(xs[:4]), pack(xs[4:])
    xa, xb = around(xa, "y"), [xb, ring(xb, X, 4, 1), ring(xb, X, 4, -1)]
    shares, xb[1], xb[2] = barrier((shares, xb[1], xb[2]))
    tiles = total(shares)
    tiles, opposite = barrier((tiles, xb[0]))
    xb.append(ring(opposite, X, 4, 2))
    tiles = swap_all(tiles)
    parts = swap_all(decode(place, cache_lengths, tiles, key_cache, value_cache))

    near = jnp.arange(16, dtype=jnp.int32)
    stored = jnp.stack([xl * 16 + near, (1 - xl) * 16 + near], axis=1).reshape(COUNT)
    logical = jnp.sum(jnp.where(chain_order[None, :] == stored[:, None], blocks[None, :], 0), axis=1)
    weights = weights.reshape(8, 4 * ROWS, HALF)
    theirs = project(PARTNER, place, logical, xa, xb, weights)
    theirs, parts = barrier((theirs, parts))
    other = ring(theirs, "xl", 2, 1)
    done = combine(parts)
    mine = project(OWN, place, logical, xa, xb, weights)
    attn_pre = prefill(place, mine, other)
    attn_dec = swap_all(done)[: BATCH // 2].reshape(BATCH, WIDTH)
    return attn_pre, attn_dec


def solution(mesh):
    fine = Mesh(np.asarray(mesh.devices).reshape(2, 8, 2, 2, 4), ("xl", "z", "c", "xh", "y"))
    rep, tp = REP, ("xh", "y")
    in_specs = (P(rep, tp), P(None, tp), P(rep, tp), P(rep, tp), P(None, rep, tp), P(None, rep, tp), P(), P())
    out_specs = (P(rep, tp), P(None, tp))
    return jax.shard_map(per_device, mesh=fine, in_specs=in_specs, out_specs=out_specs, check_vma=False)
```

```python
import functools
import math

import jax
import jax.numpy as jnp
import numpy as np
from jax import lax
from jax.experimental import pallas as pl
from jax.experimental.pallas import tpu as pltpu
from jax.sharding import Mesh
from jax.sharding import PartitionSpec as P

HD = 128
SEQ_LEN = 128
HEADS = 8
BATCH = 48
ROWS = 256
WIDTH = 1024
HALF = 640
COUNT = 32
SCALE = 1.0 / math.sqrt(HD)
REP = ("xl", "z", "c")
X = ("xl", "xh")
STEPS = (0, 3, 1, 2)
OWN, PARTNER = (0, 3), (1, 2)
negative_big = -1e30
f32 = jnp.float32


def flat_x(x):
    return (x % 2) * 2 + x // 2


def ring(value, axes, size, shift):
    pairs = [(i, (i + shift) % size) for i in range(size)]
    if axes == X:
        pairs = [(flat_x(i), flat_x(j)) for i, j in pairs]
    return lax.ppermute(value, axes, pairs)


def around(value, axes):
    return [value, ring(value, axes, 4, 1), ring(value, axes, 4, -1), ring(value, axes, 4, 2)]


def vmem(count):
    return [pl.BlockSpec(memory_space=pltpu.VMEM)] * count


def smem(count):
    return [pl.BlockSpec(memory_space=pltpu.SMEM)] * count


def anywhere(count):
    return [pl.BlockSpec(memory_space=pl.ANY)] * count


def params(mebibytes=12):
    return pltpu.CompilerParams(vmem_limit_bytes=mebibytes * 1024 * 1024)


def shaped(dtype, *shape):
    return jax.ShapeDtypeStruct(shape, dtype)


bf16 = functools.partial(shaped, jnp.bfloat16)


def split_kernel(place_ref, qw_ref, kv_ref, kept_ref, given_ref, sems):
    def write(left_ref, right_ref):
        copies = [
            pltpu.make_async_copy(qw_ref.at[:, :512], left_ref.at[:, :512], sems.at[0]),
            pltpu.make_async_copy(kv_ref.at[:, :HD], left_ref.at[:, 512:], sems.at[1]),
            pltpu.make_async_copy(qw_ref.at[:, 512:], right_ref.at[:, :512], sems.at[2]),
            pltpu.make_async_copy(kv_ref.at[:, HD:], right_ref.at[:, 512:], sems.at[3]),
        ]
        for copy in copies:
            copy.start()
        for copy in copies:
            copy.wait()

    @pl.when(place_ref[0] == 0)
    def _():
        write(kept_ref, given_ref)

    @pl.when(place_ref[0] != 0)
    def _():
        write(given_ref, kept_ref)


def split(place, qw, kv):
    return pl.pallas_call(
        split_kernel,
        in_specs=smem(1) + anywhere(2),
        out_specs=anywhere(2),
        out_shape=[bf16(ROWS, HALF)] * 2,
        scratch_shapes=[pltpu.SemaphoreType.DMA((4,))],
        compiler_params=params(),
        name="split",
    )(place, qw, kv)


def pack_kernel(*refs):
    row = 0
    for ref in refs[:-1]:
        refs[-1][row : row + ref.shape[0]] = ref[...]
        row += ref.shape[0]


def pack(parts):
    return pl.pallas_call(
        pack_kernel,
        in_specs=vmem(len(parts)),
        out_specs=pl.BlockSpec(memory_space=pltpu.VMEM),
        out_shape=bf16(sum(v.shape[0] for v in parts), parts[0].shape[1]),
        compiler_params=params(),
        name="pack",
    )(*parts)


def project_kernel(slots, place_ref, logical_ref, *refs):
    a_refs, b_refs, w_ref, out_ref = refs[:4], refs[4:8], refs[8], refs[9]
    x_all, w_all, acc, x_sem, w_sem = refs[10:]
    x, y = place_ref[1], place_ref[2]
    copies = []
    for n, slot in enumerate(slots):
        at_x = (x + STEPS[slot]) % 4
        for i in range(4):
            at_y = (y + STEPS[i]) % 4
            group = (at_x // 2) * 4 + at_y
            copies.append((a_refs[i].at[slot * 128 : (slot + 1) * 128], x_all.at[group, :128], 2 * (4 * n + i)))
            copies.append((b_refs[slot].at[i * 128 : (i + 1) * 128], x_all.at[group, 128:], 2 * (4 * n + i) + 1))
    copies = [pltpu.make_async_copy(src, dst, x_sem.at[s]) for src, dst, s in copies]
    loads = [pltpu.make_async_copy(w_ref.at[i], w_all.at[i], w_sem.at[i]) for i in range(8)]
    for copy in copies + loads:
        copy.start()
    for copy in copies:
        copy.wait()
    for i in range(8):
        loads[i].wait()
        lhs = []
        for k in range(4):
            block = logical_ref[4 * i + k]
            lhs.append(x_all[block // 4, :, pl.ds(pl.multiple_of((block % 4) * ROWS, ROWS), ROWS)])
        part = jnp.dot(jnp.concatenate(lhs, axis=1), w_all[i], preferred_element_type=f32)
        if i == 0:
            acc[...] = part
        elif i < 7:
            acc[...] += part
        else:
            out_ref[...] = (acc[...] + part).astype(out_ref.dtype)


def project(slots, place, logical, a, b, w):
    return pl.pallas_call(
        functools.partial(project_kernel, slots),
        in_specs=smem(2) + anywhere(9),
        out_specs=pl.BlockSpec(memory_space=pltpu.VMEM),
        out_shape=bf16(ROWS, HALF),
        scratch_shapes=[
            pltpu.VMEM((8, ROWS, WIDTH), jnp.bfloat16),
            pltpu.VMEM((8, 4 * ROWS, HALF), jnp.bfloat16),
            pltpu.VMEM((ROWS, HALF), f32),
            pltpu.SemaphoreType.DMA((16,)),
            pltpu.SemaphoreType.DMA((8,)),
        ],
        compiler_params=params(48),
        cost_estimate=pl.CostEstimate(flops=2 * ROWS * 8192 * HALF, bytes_accessed=15_000_000, transcendentals=0),
        name="project",
    )(place, logical, *a, *b, w)


def prefill_kernel(place_ref, mine_ref, other_ref, decode_ref, out_ref, decode_out_ref, rows_ref):
    rows_ref[...] = decode_ref[: BATCH // 2].astype(f32).reshape(BATCH, HEADS, HD)
    for head in range(HEADS):
        decode_out_ref[:, head * HD : (head + 1) * HD] = rows_ref[:, head, :].astype(decode_out_ref.dtype)
    first = place_ref[0] == 0
    mine, other = mine_ref[...], other_ref[...]
    low = jnp.where(first, mine, other)
    high = jnp.where(first, other, mine)
    row = lax.broadcasted_iota(jnp.int32, (SEQ_LEN, SEQ_LEN), 0)
    col = lax.broadcasted_iota(jnp.int32, (SEQ_LEN, SEQ_LEN), 1)
    causal = row >= col
    causal = jnp.concatenate([causal] * HEADS, axis=0)
    for n in range(ROWS // SEQ_LEN):
        at = slice(n * SEQ_LEN, (n + 1) * SEQ_LEN)
        keys, values = low[at, 512:], high[at, 512:]
        queries = [part[at, h * HD : (h + 1) * HD] for part in (low, high) for h in range(4)]
        scores = lax.dot_general(
            jnp.concatenate(queries, axis=0), keys, (((1,), (1,)), ((), ())), preferred_element_type=f32
        ) * SCALE
        scores = jnp.where(causal, scores, negative_big)
        expos = jnp.exp(scores - jnp.max(scores, axis=-1, keepdims=True))
        sums = jnp.sum(expos, axis=-1, keepdims=True)
        weighted = (jnp.dot(expos.astype(jnp.bfloat16), values, preferred_element_type=f32) / sums).astype(jnp.bfloat16)
        for head in range(HEADS):
            out_ref[at, head * HD : (head + 1) * HD] = weighted[head * SEQ_LEN : (head + 1) * SEQ_LEN]


def prefill(place, mine, other, decoded):
    return pl.pallas_call(
        prefill_kernel,
        in_specs=smem(1) + vmem(3),
        out_specs=vmem(2),
        out_shape=[bf16(ROWS, WIDTH), bf16(BATCH, WIDTH)],
        scratch_shapes=[pltpu.VMEM((BATCH, HEADS, HD), f32)],
        compiler_params=params(),
        cost_estimate=pl.CostEstimate(flops=140_000_000, bytes_accessed=1_200_000, transcendentals=262144),
        name="prefill_attention",
    )(place, mine, other, decoded)


def partial_kernel(x_ref, qw_ref, kv_ref, out_ref):
    x = x_ref[...]
    for col, part in ((0, jnp.dot(x, qw_ref[...], preferred_element_type=f32)), (8, jnp.dot(x, kv_ref[...], preferred_element_type=f32))):
        for i in range(BATCH // 8):
            for j in range(part.shape[1] // HD):
                out_ref[i * 10 + col + j] = part[i * 8 : (i + 1) * 8, j * HD : (j + 1) * HD]
    out_ref[60:] = jnp.zeros((4, 8, HD), f32)


def partial(x, qw, kv):
    return pl.pallas_call(
        partial_kernel,
        in_specs=vmem(3),
        out_specs=pl.BlockSpec(memory_space=pltpu.VMEM),
        out_shape=shaped(f32, 64, 8, HD),
        compiler_params=params(),
        name="decode_partial",
    )(x, qw, kv)


def total_kernel(in_ref, out_ref):
    both = [jnp.sum(in_ref[:, m], axis=0) for m in range(2)]
    done = jnp.concatenate(both, axis=0).astype(jnp.bfloat16)
    out_ref[...] = jnp.broadcast_to(done[None], out_ref.shape)


def total(shares):
    return pl.pallas_call(
        total_kernel,
        in_specs=vmem(1),
        out_specs=pl.BlockSpec(memory_space=pltpu.VMEM),
        out_shape=bf16(COUNT, 16, HD),
        compiler_params=params(),
        name="decode_total",
    )(shares.reshape(COUNT, 2, 8, HD))


def decode_kernel(place_ref, length_ref, tile_ref, key_hbm, value_hbm, out_ref, rows_ref, score_ref, length_rows, key_ref, value_ref, sems):
    loads = [pltpu.make_async_copy(key_hbm, key_ref, sems.at[0]), pltpu.make_async_copy(value_hbm, value_ref, sems.at[1])]
    for load in loads:
        load.start()
    rep = place_ref[3]
    with_own = rep == 0
    for i in range(BATCH // 8):
        for j in range(10):
            t = i * 10 + j
            tile = tile_ref[t // 2, (t % 2) * 8 : (t % 2 + 1) * 8, :].astype(f32)
            rows_ref[i * 8 : (i + 1) * 8, j, :] = tile
    loads[0].wait()
    for b in range(BATCH):
        score_ref[b] = lax.dot_general(
            rows_ref[b, 0:8].astype(jnp.bfloat16), key_ref[b], (((1,), (1,)), ((), ())), preferred_element_type=f32
        )
        length_rows[b] = jnp.full((8, HD), length_ref[b], jnp.int32)
    lane = lax.broadcasted_iota(jnp.int32, (8, HD), 1)
    position = (rep * key_ref.shape[1] + lane)[None]
    loads[1].wait()
    for i in range(BATCH // 8):
        at = slice(i * 8, (i + 1) * 8)
        scores = score_ref[at] * SCALE
        own = jnp.sum(rows_ref[at, 0:8] * rows_ref[at, 8:9], axis=-1, keepdims=True) * SCALE
        allowed = position < length_rows[at]
        own = jnp.where(with_own, own, negative_big)
        top = jnp.maximum(jnp.max(jnp.where(allowed, scores, negative_big), axis=-1, keepdims=True), own)
        expos = jnp.where(allowed, jnp.exp(scores - top), 0.0)
        own_exp = jnp.where(with_own, jnp.exp(own - top), 0.0)
        sums = jnp.sum(expos, axis=-1, keepdims=True) + own_exp
        extra = own_exp.astype(jnp.bfloat16).astype(f32) * rows_ref[at, 9:10]
        weights = expos.astype(jnp.bfloat16)
        for k in range(0, 8, 2):
            pair = (i * 8 + k) // 2
            for m in range(2):
                outs = jnp.dot(weights[k + m], value_ref[i * 8 + k + m], preferred_element_type=f32)
                out_ref[pair, 8 * m : 8 * (m + 1)] = outs + extra[k + m]
            stats = jnp.where(lane == 0, top[k], jnp.where(lane == 1, sums[k], 1.0))
            out_ref[pair, 16:24] = jnp.where(lane == 2, top[k + 1], jnp.where(lane == 3, sums[k + 1], stats))
    out_ref[BATCH // 2 :] = jnp.ones((COUNT - BATCH // 2, 24, HD), f32)


def decode(place, lengths, tiles, keys, values):
    return pl.pallas_call(
        decode_kernel,
        in_specs=smem(2) + vmem(1) + anywhere(2),
        out_specs=pl.BlockSpec(memory_space=pltpu.VMEM),
        out_shape=shaped(f32, COUNT, 24, HD),
        scratch_shapes=[
            pltpu.VMEM((BATCH, 16, HD), f32),
            pltpu.VMEM((BATCH, 8, HD), f32),
            pltpu.VMEM((BATCH, 8, HD), jnp.int32),
            pltpu.VMEM((BATCH, HD, HD), jnp.bfloat16),
            pltpu.VMEM((BATCH, HD, HD), jnp.bfloat16),
            pltpu.SemaphoreType.DMA((2,)),
        ],
        compiler_params=params(56),
        cost_estimate=pl.CostEstimate(flops=30_000_000, bytes_accessed=4_000_000, transcendentals=50000),
        name="decode_attention",
    )(place, lengths, tiles, keys, values)


def combine_kernel(in_ref, out_ref):
    stats = in_ref[:, 16:24]
    done = []
    for m in range(2):
        tops, sums = stats[:, :, 2 * m : 2 * m + 1], stats[:, :, 2 * m + 1 : 2 * m + 2]
        keep = jnp.exp(tops - jnp.max(tops, axis=0, keepdims=True))
        numer = jnp.sum(in_ref[:, 8 * m : 8 * (m + 1)] * keep, axis=0)
        done.append(numer / jnp.sum(sums * keep, axis=0))
    done = jnp.concatenate(done, axis=0).astype(jnp.bfloat16)
    out_ref[...] = jnp.broadcast_to(done[None], out_ref.shape)


def combine(parts):
    return pl.pallas_call(
        combine_kernel,
        in_specs=vmem(1),
        out_specs=pl.BlockSpec(memory_space=pltpu.VMEM),
        out_shape=bf16(COUNT, 16, HD),
        compiler_params=params(),
        name="decode_combine",
    )(parts)


def swap_all(value):
    return lax.all_to_all(value, REP, 0, 0, tiled=True)


def per_device(prefill_x, decode_x, query_weight, keyvalue_weight, key_cache, value_cache, cache_lengths, chain_order):
    xl, z, c = lax.axis_index("xl"), lax.axis_index("z"), lax.axis_index("c")
    xh, y = lax.axis_index("xh"), lax.axis_index("y")
    x = xh * 2 + xl
    rep = xl * 16 + z * 2 + c
    place = jnp.stack([xl, x, y, rep]).astype(jnp.int32)
    blocks = jnp.arange(COUNT, dtype=jnp.int32)

    barrier = lax.optimization_barrier
    block = jnp.sum(jnp.where(chain_order == rep, blocks, 0))
    piece_x = lax.dynamic_slice(decode_x, (0, (block % 4) * ROWS), (BATCH, ROWS))
    piece_x = jnp.where(block // 4 == xh * 4 + y, piece_x, jnp.zeros_like(piece_x))

    kept, given = split(place, query_weight, keyvalue_weight)
    got = ring(given, "xl", 2, 1)
    xb = around(prefill_x[128:], "y")
    piece_x = piece_x + ring(piece_x, "xh", 2, 1)
    got, piece_x, xb[1], xb[2] = barrier((got, piece_x, xb[1], xb[2]))
    weights = lax.all_gather(jnp.stack([kept, got]), ("z", "c"))

    piece_x = piece_x + ring(piece_x, "y", 4, 1) + ring(piece_x, "y", 4, -1) + ring(piece_x, "y", 4, 2)
    xa = around(prefill_x[:128], X)
    shares = partial(piece_x, query_weight, keyvalue_weight)
    shares, *xs = barrier((shares, *xa, *xb))
    shares = swap_all(shares)

    xa, xb = pack(xs[:4]), pack(xs[4:])
    xa, xb = around(xa, "y"), [xb, ring(xb, X, 4, 1), ring(xb, X, 4, -1)]
    shares, xb[1], xb[2] = barrier((shares, xb[1], xb[2]))
    tiles = total(shares)
    tiles, opposite = barrier((tiles, xb[0]))
    xb.append(ring(opposite, X, 4, 2))
    tiles = swap_all(tiles)
    parts = swap_all(decode(place, cache_lengths, tiles, key_cache, value_cache))

    near = jnp.arange(16, dtype=jnp.int32)
    stored = jnp.stack([xl * 16 + near, (1 - xl) * 16 + near], axis=1).reshape(COUNT)
    logical = jnp.sum(jnp.where(chain_order[None, :] == stored[:, None], blocks[None, :], 0), axis=1)
    weights = weights.reshape(8, 4 * ROWS, HALF)
    theirs = project(PARTNER, place, logical, xa, xb, weights)
    theirs, parts = barrier((theirs, parts))
    other = ring(theirs, "xl", 2, 1)
    done = combine(parts)
    mine = project(OWN, place, logical, xa, xb, weights)
    attn_pre, attn_dec = prefill(place, mine, other, swap_all(done))
    return attn_pre, attn_dec


def solution(mesh):
    fine = Mesh(np.asarray(mesh.devices).reshape(2, 8, 2, 2, 4), ("xl", "z", "c", "xh", "y"))
    rep, tp = REP, ("xh", "y")
    in_specs = (P(rep, tp), P(None, tp), P(rep, tp), P(rep, tp), P(None, rep, tp), P(None, rep, tp), P(), P())
    out_specs = (P(rep, tp), P(None, tp))
    return jax.shard_map(per_device, mesh=fine, in_specs=in_specs, out_specs=out_specs, check_vma=False)
```
